512 devices in a mesh: grp: 32 (over z, core), own: 16 (over y, x).
Axes of the slice: x: 4, y: 4, z: 16, core: 2. Of those that a mesh axis runs over, the one named last changes fastest.
Arguments:
- multipoles: bfloat16 [289, 65536], P(None, ('grp', 'own')), may hold values from -6 to 6
- operators: bfloat16 [320, 289, 289], P('own'), may hold values from -0.02734375 to 0.02734375
- targets: int32 [98304, 1], P(('grp', 'own')), may hold values from 0 to 15; in each aligned block of 3072 rows (0 to 3071, 3072 to 6143, ...) at most 288 rows name the same one
- sources: int32 [98304], P(('grp', 'own')), may hold values from 0 to 47
- classes: int32 [98304], P(('grp', 'own')), may hold values from 0 to 319, as said below
- owners: int32 [32, 16], P('grp'), may hold values from 0 to 15, each once within a row
Outputs:
- local_exp: float32 [289, 65536], P(None, ('grp', 'own'))
The draws below stay inside these ranges and needn't reach their ends.
Inputs may be any that keep to these rules, and one draw needn't show every extreme that they name: `targets`: in each group's 3072 pairs no target block is named by more than 288 pairs; some group has a target named by exactly 288. `classes`: pair i has a class from o * 20 to (o + 1) * 20 - 1, where o = (i // 192) % 16. `owners`: each row is a permutation of 0 to 16 - 1.
All inputs are finite; a program needn't handle non-finite values.
Results may differ from the reference program's by a relative error of at most 0.0003.
Values may be sent and summed in bfloat16 or wider, within the bound.
No kernel may reach another device: no remote copies, remote signals or barrier semaphores. Data moves between devices by JAX's collectives and lax.ppermute only.
A program may use at most 64 MiB of HBM per device.

```python
import math
import jax
import jax.numpy as jnp
import numpy as np
from jax import lax

P_SIZE = 289
BLOCK = 128
OPS = 320
PAIRS_DEV = 192
MOST = 288
NPG = 3072
PAIRS = 98304
BOXES = 65536
N_GRP = 32
N_OWN = 16


def draw_classes(key, part):
    key = jax.random.fold_in(key, 7)
    ops_dev = OPS // N_OWN
    total = PAIRS_DEV * N_OWN * N_GRP
    index = jnp.arange(total, dtype=jnp.int32)
    holder = index // PAIRS_DEV % N_OWN
    within = jax.random.randint(key, (total,), 0, ops_dev, dtype=jnp.int32)
    return (holder * ops_dev + within).astype(jnp.int32)


def with_ends(entries, own_key, smallest, top_value):
    dims = entries.shape
    index_at = [jax.random.randint(jax.random.fold_in(own_key, axis), (), 0, dims[axis]) for axis in range(len(dims))]
    entries = entries.at[tuple(index_at)].set(smallest)
    longest = dims.index(max(dims))
    index_at[longest] = (index_at[longest] + 1) % dims[longest]
    return entries.at[tuple(index_at)].set(top_value)


def level_of(rng, shape, split, smallest, top_value):
    factor_of = 1.0
    for position, shards_of in split:
        steps = jax.random.uniform(jax.random.fold_in(jax.random.fold_in(rng, 6), position), (shards_of,), jnp.float32, smallest / len(split), top_value / len(split))
        factor_of = factor_of * jnp.repeat(jnp.exp(steps), shape[position] // shards_of).reshape((-1,) + (1,) * (len(shape) - 1 - position))
    return factor_of


def deal_out(rng, own, number, rows, count, top, limit, skew):
    ranking = jax.random.permutation(rng, count)
    crowded, usual = portions_of(count, rows * top, limit, skew, True), portions_of(count, rows * top, limit, skew, False)
    places = jnp.arange(count)

    def named(sizes, offset_by):
        used = int((sizes > 0).sum())
        fixed = max(1, used // 4)
        moved = fixed + (places - fixed + offset_by * (used - fixed)) % max(1, count - fixed)
        return jnp.zeros((count,), jnp.int32).at[ranking[jnp.where(places < fixed, places, moved)]].set(jnp.asarray(sizes, jnp.int32))

    sizes = jnp.where(number % 4 == 0, named(crowded, number // 4), named(usual, number - number // 4 - 1))
    mixed = jax.random.permutation(jax.random.fold_in(own, 3), count)
    source_of, taker = mixed[0:count // 2 * 2:2], mixed[1:count // 2 * 2:2]
    margin = jnp.minimum(sizes[source_of] - 1, limit - sizes[taker]) // 2
    margin = jnp.where((source_of == ranking[0]) | (taker == ranking[0]) | (sizes[taker] == 0), 0, jnp.maximum(margin, 0))
    moved = jax.random.randint(jax.random.fold_in(own, 4), (count // 2,), 0, 1 << 20) % (margin + 1)
    sizes = sizes.at[source_of].add(-moved).at[taker].add(moved)
    labels = jnp.searchsorted(jnp.cumsum(sizes), jnp.arange(rows * top), side="right").astype(jnp.int32)
    table = labels.reshape(top, rows).T
    table = table[jax.random.permutation(jax.random.fold_in(own, 1), rows)]
    offset_by = jax.random.randint(jax.random.fold_in(own, 2), (rows, 1), 0, top)
    return jnp.take_along_axis(table, (jnp.arange(top)[None, :] + offset_by) % top, axis=1)


def portions_of(amount, total, reach, slope, full):
    loads = [(1 << 20) // math.isqrt(grade ** slope) + 1 for grade in range(1, amount + 1)]
    largest = reach if full else min(reach, max(-(-total // amount), total * loads[0] // sum(loads)))
    least = 1 if total - largest >= amount - 1 else 0
    given, rest = [largest] + [least] * (amount - 1), total - largest - least * (amount - 1)
    while rest > 0:
        candidates = [i for i in range(1, amount) if given[i] < largest] or [i for i in range(1, amount) if given[i] < reach]
        mass, left = sum([loads[i] for i in candidates]), rest
        for i in candidates:
            extra = min(reach - given[i], max(1, left * loads[i] // mass), rest)
            given[i] = given[i] + extra
            rest = rest - extra
    return np.array(given)


def noise(rng, shape, deviation, reach, pieces=(), kind=jnp.bfloat16):
    drawn = deviation * jax.random.normal(rng, shape, jnp.float32)
    if pieces:
        drawn = drawn * level_of(rng, shape, pieces, -0.22, 0.18)
    return jnp.clip(drawn, -reach, reach).astype(kind)


def setup_inputs(seed: int = 0) -> dict:
    streams_of = jax.random.split(jax.random.key(seed), 7)
    multipoles = noise(streams_of[0], (P_SIZE, BOXES), 1.0, 6.0, ((1, 512),))
    operators = noise(streams_of[1], (OPS, P_SIZE, P_SIZE), (P_SIZE * PAIRS_DEV) ** -0.5, 0.02734375, ((0, 16),))
    targets_keys = jax.random.split(jax.random.fold_in(streams_of[2], 1), PAIRS // NPG)
    targets_turns = jax.random.permutation(jax.random.fold_in(streams_of[2], 3), PAIRS // NPG)
    targets = jax.vmap(lambda own, number: deal_out(jax.random.fold_in(streams_of[2], 2), own, number, NPG, N_OWN, 1, MOST, 2))(targets_keys, targets_turns).reshape((PAIRS, 1))
    sources = with_ends(jax.random.randint(streams_of[3], (PAIRS,), 0, 3 * N_OWN), jax.random.fold_in(streams_of[3], 1), 0, (3 * N_OWN) - 1).astype(jnp.int32)
    classes = draw_classes(jax.random.fold_in(streams_of[6], 71), 0)
    owners = jax.vmap(lambda own: jax.random.permutation(own, N_OWN))(jax.random.split(streams_of[5], N_GRP)).reshape((N_GRP, N_OWN)).astype(jnp.int32)
    return dict(multipoles=multipoles, operators=operators, targets=targets, sources=sources, classes=classes, owners=owners)


def reference(multipoles, operators, targets, sources, classes, owners):
    own_n = N_OWN
    groups = N_GRP
    npg = PAIRS_DEV * N_OWN
    step_n = 32
    cols = multipoles.astype(jnp.float32).reshape(P_SIZE, groups, own_n, BLOCK)
    padded = jnp.pad(cols, ((0, 0), (1, 1), (0, 0), (0, 0)))
    tgt = targets[:, 0].reshape(groups, npg // step_n, step_n)
    src = sources.reshape(groups, npg // step_n, step_n)
    cls = classes.reshape(groups, npg // step_n, step_n)
    ops_wide = operators.astype(jnp.float32)

    def one_group(items):
        group_id, tgt_row, src_row, cls_row, perm = items
        near = lax.dynamic_slice_in_dim(padded, group_id, 3, 1)
        panel = jnp.transpose(near, (2, 1, 0, 3)).reshape(3 * own_n, P_SIZE, BLOCK)

        def add_pairs(total, part):
            tgt_blk, src_blk, cls_blk = part
            mats = jnp.take(ops_wide, cls_blk, axis=0)
            picked = jnp.take(panel, src_blk, axis=0)
            contrib = jnp.einsum('nqp,npb->nqb', mats, picked, precision=lax.Precision.HIGHEST)
            return total.at[tgt_blk].add(contrib), None

        start = jnp.zeros((own_n, P_SIZE, BLOCK), jnp.float32)
        total, unused = lax.scan(add_pairs, start, (tgt_row, src_row, cls_row))
        return jnp.zeros((own_n, P_SIZE, BLOCK), jnp.float32).at[perm].set(total)

    result = lax.map(one_group, (jnp.arange(groups, dtype=jnp.int32), tgt, src, cls, owners))
    return jnp.transpose(result, (2, 0, 1, 3)).reshape(P_SIZE, groups * own_n * BLOCK)
```

```python
import jax
import jax.numpy as jnp
from jax import lax
from jax.experimental import pallas as pl
from jax.experimental.pallas import tpu as pltpu
from jax.sharding import PartitionSpec as P

GROUP = 8
SLOTS = 256
VMEM = pl.BlockSpec(memory_space=pltpu.VMEM)
SMEM = pl.BlockSpec(memory_space=pltpu.SMEM)


def plan(target, sources, classes, owners, held):
    count = target.shape[0]
    own_n = owners.shape[0]
    odd = lax.rem(lax.axis_index("grp"), 2)
    shift = sources % 3
    kind = jnp.where(shift == 1, 0, jnp.where((shift == 0) == (odd == 0), 2, 1))
    local = classes - lax.axis_index("own") * held
    dest = jnp.sum(jnp.where(target[:, None] == jnp.arange(own_n)[None, :], owners[None, :], 0), axis=1)
    packed = local + 32 * (sources // 3) + 2048 * dest
    run = kind * held + local
    pos = jnp.arange(count)
    rank = jnp.sum((run[:, None] == run[None, :]) & (pos[None, :] < pos[:, None]), axis=1, dtype=jnp.int32)
    runs = jnp.arange(3 * held)
    length = jnp.sum(run[:, None] == runs[None, :], axis=0, dtype=jnp.int32)
    length = (length + 1) // 2 * 2
    offset = jnp.sum(jnp.where(runs[None, :] < run[:, None], length[None, :], 0), axis=1)
    slot = offset + rank
    empty = 2048 * own_n
    items = empty + jnp.sum(jnp.where(slot[None, :] == jnp.arange(SLOTS)[:, None], packed[None, :] - empty, 0), axis=1)
    ends = jnp.sum(jnp.where(runs[None, :] < held * jnp.arange(1, 4)[:, None], length[None, :], 0), axis=1) // 2
    return items.astype(jnp.int32), ends.astype(jnp.int32)


def add_items(items, first, last, operators, panel, total):
    coeffs = operators.shape[1]

    def one(i):
        left, right = items[2 * i], items[2 * i + 1]
        both = jnp.concatenate([panel[(left >> 5) & 63][:coeffs], panel[(right >> 5) & 63][:coeffs]], axis=1)
        made = jnp.dot(operators[left & 31], both, preferred_element_type=jnp.float32)
        return made, left >> 11, right >> 11

    def put(made, left, right):
        total[left, :coeffs] += made[:, :128]
        total[right, :coeffs] += made[:, 128:]

    def many(k, carry):
        for part in [one(first + k * GROUP + u) for u in range(GROUP)]:
            put(*part)
        return carry

    def single(i, carry):
        put(*one(i))
        return carry

    full = lax.div(last - first, GROUP)
    lax.fori_loop(0, full, many, 0)
    lax.fori_loop(first + full * GROUP, last, single, 0)


def near_kernel(items, ends, operators, own_panel, other_panel, total):
    total[...] = jnp.zeros_like(total)
    add_items(items, 0, ends[0], operators, own_panel, total)
    add_items(items, ends[0], ends[1], operators, other_panel, total)


def far_kernel(items, ends, operators, panel, begun, out, total):
    total[...] = begun[...]
    add_items(items, ends[1], ends[2], operators, panel, total)
    out[...] = total[: out.shape[0]]


def per_device(multipoles, operators, targets, sources, classes, owners):
    own_n = lax.axis_size("own")
    grp_n = lax.axis_size("grp")
    coeffs, width = multipoles.shape
    held = operators.shape[0]
    rows = (coeffs + 15) // 16 * 16
    sums = (coeffs + 7) // 8 * 8
    padded = jnp.pad(multipoles, ((0, rows - coeffs), (0, 0)))
    own_panel = lax.all_to_all(
        jnp.broadcast_to(padded, (own_n, rows, width)), "own", split_axis=0, concat_axis=0, tiled=True
    )
    across = [(i, i + 1) for i in range(1, grp_n - 1, 2)]
    far_panel = lax.ppermute(own_panel, "grp", across + [(j, i) for i, j in across])
    other_panel = lax.ppermute(own_panel, "grp", [(i, i ^ 1) for i in range(grp_n)])
    target, sources, classes, owner, unused = lax.optimization_barrier(
        (targets[:, 0], sources, classes, owners[0], own_panel)
    )
    items, ends = plan(target, sources, classes, owner, held)
    vmem = pltpu.CompilerParams(vmem_limit_bytes=32 * 2**20)
    pair = 2 * coeffs * coeffs * width
    begun = pl.pallas_call(
        near_kernel,
        out_shape=jax.ShapeDtypeStruct((own_n + 1, sums, width), jnp.float32),
        in_specs=[SMEM, SMEM, VMEM, VMEM, VMEM],
        out_specs=VMEM,
        compiler_params=vmem,
        cost_estimate=pl.CostEstimate(flops=3 * 128 * pair, bytes_accessed=2**23, transcendentals=0),
    )(items, ends, operators, own_panel, other_panel)
    partial = pl.pallas_call(
        far_kernel,
        out_shape=jax.ShapeDtypeStruct((own_n, sums, width), jnp.float32),
        in_specs=[SMEM, SMEM, VMEM, VMEM, VMEM],
        out_specs=VMEM,
        scratch_shapes=[pltpu.VMEM((own_n + 1, sums, width), jnp.float32)],
        compiler_params=vmem,
        cost_estimate=pl.CostEstimate(flops=3 * 64 * pair, bytes_accessed=2**23, transcendentals=0),
    )(items, ends, operators, far_panel, begun)
    moved = lax.all_to_all(partial, "own", split_axis=0, concat_axis=0, tiled=True)
    return jnp.sum(moved, axis=0)[:coeffs]


def solution(mesh):
    placed = (
        P(None, ("grp", "own")),
        P("own", None, None),
        P(("grp", "own"), None),
        P(("grp", "own")),
        P(("grp", "own")),
        P("grp", None),
    )
    return jax.shard_map(
        per_device, mesh=mesh, in_specs=placed, out_specs=P(None, ("grp", "own")), check_vma=False
    )
```

```python
import jax
import jax.numpy as jnp
from jax import lax
from jax.experimental import pallas as pl
from jax.experimental.pallas import tpu as pltpu
from jax.sharding import PartitionSpec as P

GROUP = 8
SLOTS = 256
LEVELS = 32000.0
FINE = 64.0
VMEM = pl.BlockSpec(memory_space=pltpu.VMEM)
SMEM = pl.BlockSpec(memory_space=pltpu.SMEM)


def plan(target, sources, classes, owners, held):
    count = target.shape[0]
    own_n = owners.shape[0]
    odd = lax.rem(lax.axis_index("grp"), 2)
    shift = sources % 3
    kind = jnp.where(shift == 1, 0, jnp.where((shift == 0) == (odd == 0), 2, 1))
    local = classes - lax.axis_index("own") * held
    dest = jnp.sum(jnp.where(target[:, None] == jnp.arange(own_n)[None, :], owners[None, :], 0), axis=1)
    packed = local + 32 * (sources // 3) + 2048 * dest
    run = kind * held + local
    pos = jnp.arange(count)
    rank = jnp.sum((run[:, None] == run[None, :]) & (pos[None, :] < pos[:, None]), axis=1, dtype=jnp.int32)
    runs = jnp.arange(3 * held)
    length = jnp.sum(run[:, None] == runs[None, :], axis=0, dtype=jnp.int32)
    length = (length + 1) // 2 * 2
    offset = jnp.sum(jnp.where(runs[None, :] < run[:, None], length[None, :], 0), axis=1)
    slot = offset + rank
    empty = 2048 * own_n
    items = empty + jnp.sum(jnp.where(slot[None, :] == jnp.arange(SLOTS)[:, None], packed[None, :] - empty, 0), axis=1)
    ends = jnp.sum(jnp.where(runs[None, :] < held * jnp.arange(1, 4)[:, None], length[None, :], 0), axis=1) // 2
    return items.astype(jnp.int32), ends.astype(jnp.int32)


def add_items(items, first, last, operators, panel, total):
    coeffs = operators.shape[1]

    def one(i):
        left, right = items[2 * i], items[2 * i + 1]
        both = jnp.concatenate([panel[(left >> 5) & 63][:coeffs], panel[(right >> 5) & 63][:coeffs]], axis=1)
        made = jnp.dot(operators[left & 31], both, preferred_element_type=jnp.float32)
        return made, left >> 11, right >> 11

    def put(made, left, right):
        total[left, :coeffs] += made[:, :128]
        total[right, :coeffs] += made[:, 128:]

    def many(k, carry):
        for part in [one(first + k * GROUP + u) for u in range(GROUP)]:
            put(*part)
        return carry

    def single(i, carry):
        put(*one(i))
        return carry

    full = lax.div(last - first, GROUP)
    lax.fori_loop(0, full, many, 0)
    lax.fori_loop(first + full * GROUP, last, single, 0)


def near_kernel(items, ends, operators, own_panel, other_panel, total):
    total[...] = jnp.zeros_like(total)
    add_items(items, 0, ends[0], operators, own_panel, total)
    add_items(items, ends[0], ends[1], operators, other_panel, total)


def far_kernel(items, ends, operators, panel, begun, out, total):
    coeffs = operators.shape[1]
    total[...] = begun[...]
    add_items(items, ends[1], ends[2], operators, panel, total)

    def code(t, carry):
        values = total[t]
        top = jnp.maximum(jnp.max(jnp.abs(values), axis=0, keepdims=True), 1e-37)
        level = jnp.ceil(jnp.log2(top) * FINE)
        steps = jnp.round(values * jnp.exp2(level * (-1.0 / FINE)) * LEVELS)
        row = lax.broadcasted_iota(jnp.int32, values.shape, 0)
        out[t] = jnp.where(row < coeffs, steps, level).astype(jnp.int32).astype(jnp.int16)
        return carry

    lax.fori_loop(0, out.shape[0], code, 0)


def sum_kernel(moved, out):
    coeffs = out.shape[0]
    result = jnp.zeros(out.shape, jnp.float32)
    for j in range(moved.shape[0]):
        values = moved[j].astype(jnp.int32).astype(jnp.float32)
        scale = jnp.exp2(values[coeffs : coeffs + 1] * (1.0 / FINE)) * (1.0 / LEVELS)
        result = result + values[:coeffs] * scale
    out[...] = result


def per_device(multipoles, operators, targets, sources, classes, owners):
    own_n = lax.axis_size("own")
    grp_n = lax.axis_size("grp")
    coeffs, width = multipoles.shape
    held = operators.shape[0]
    rows = (coeffs + 16) // 16 * 16
    padded = jnp.pad(multipoles, ((0, rows - coeffs), (0, 0)))
    own_panel = lax.all_to_all(
        jnp.broadcast_to(padded, (own_n, rows, width)), "own", split_axis=0, concat_axis=0, tiled=True
    )
    across = [(i, i + 1) for i in range(1, grp_n - 1, 2)]
    far_panel = lax.ppermute(own_panel, "grp", across + [(j, i) for i, j in across])
    other_panel = lax.ppermute(own_panel, "grp", [(i, i ^ 1) for i in range(grp_n)])
    target, sources, classes, owner, unused = lax.optimization_barrier(
        (targets[:, 0], sources, classes, owners[0], own_panel)
    )
    items, ends = plan(target, sources, classes, owner, held)
    vmem = pltpu.CompilerParams(vmem_limit_bytes=32 * 2**20)
    pair = 2 * coeffs * coeffs * width
    begun = pl.pallas_call(
        near_kernel,
        out_shape=jax.ShapeDtypeStruct((own_n + 1, rows, width), jnp.float32),
        in_specs=[SMEM, SMEM, VMEM, VMEM, VMEM],
        out_specs=VMEM,
        compiler_params=vmem,
        cost_estimate=pl.CostEstimate(flops=3 * 128 * pair, bytes_accessed=2**23, transcendentals=0),
    )(items, ends, operators, own_panel, other_panel)
    partial = pl.pallas_call(
        far_kernel,
        out_shape=jax.ShapeDtypeStruct((own_n, rows, width), jnp.int16),
        in_specs=[SMEM, SMEM, VMEM, VMEM, VMEM],
        out_specs=VMEM,
        scratch_shapes=[pltpu.VMEM((own_n + 1, rows, width), jnp.float32)],
        compiler_params=vmem,
        cost_estimate=pl.CostEstimate(flops=3 * 64 * pair, bytes_accessed=2**23, transcendentals=0),
    )(items, ends, operators, far_panel, begun)
    moved = lax.all_to_all(partial, "own", split_axis=0, concat_axis=0, tiled=True)
    return pl.pallas_call(
        sum_kernel,
        out_shape=jax.ShapeDtypeStruct((coeffs, width), jnp.float32),
        in_specs=[VMEM],
        out_specs=VMEM,
        compiler_params=vmem,
    )(moved)


def solution(mesh):
    placed = (
        P(None, ("grp", "own")),
        P("own", None, None),
        P(("grp", "own"), None),
        P(("grp", "own")),
        P(("grp", "own")),
        P("grp", None),
    )
    return jax.shard_map(
        per_device, mesh=mesh, in_specs=placed, out_specs=P(None, ("grp", "own")), check_vma=False
    )
```

```python
import math

import jax
import jax.numpy as jnp
from jax import lax
from jax.experimental import pallas as pl
from jax.experimental.pallas import tpu as pltpu
from jax.sharding import PartitionSpec as P

GROUPS = (16, 4, 1)
SLOTS = 256
LEVELS = 32000.0
LEVEL_BITS = math.log2(LEVELS)
FINE = 64.0
VMEM = pl.BlockSpec(memory_space=pltpu.VMEM)
SMEM = pl.BlockSpec(memory_space=pltpu.SMEM)


def plan(target, sources, classes, owners, held):
    count = target.shape[0]
    own_n = owners.shape[0]
    odd = lax.rem(lax.axis_index("grp"), 2)
    shift = sources % 3
    kind = jnp.where(shift == 1, 0, jnp.where((shift == 0) == (odd == 0), 2, 1))
    local = classes - lax.axis_index("own") * held
    dest = jnp.sum(jnp.where(target[:, None] == jnp.arange(own_n)[None, :], owners[None, :], 0), axis=1)
    packed = local + 32 * (sources // 3) + 2048 * dest
    run = kind * held + local
    pos = jnp.arange(count)
    rank = jnp.sum((run[:, None] == run[None, :]) & (pos[None, :] < pos[:, None]), axis=1, dtype=jnp.int32)
    runs = jnp.arange(3 * held)
    length = jnp.sum(run[:, None] == runs[None, :], axis=0, dtype=jnp.int32)
    length = (length + 1) // 2 * 2
    offset = jnp.sum(jnp.where(runs[None, :] < run[:, None], length[None, :], 0), axis=1)
    slot = offset + rank
    empty = 2048 * own_n
    items = empty + jnp.sum(jnp.where(slot[None, :] == jnp.arange(SLOTS)[:, None], packed[None, :] - empty, 0), axis=1)
    ends = jnp.sum(jnp.where(runs[None, :] < held * jnp.arange(1, 4)[:, None], length[None, :], 0), axis=1) // 2
    return items.astype(jnp.int32), ends.astype(jnp.int32)


def add_items(items, first, last, operators, panel, total):
    coeffs = operators.shape[1]

    def one(i):
        left, right = items[2 * i], items[2 * i + 1]
        both = jnp.concatenate([panel[(left >> 5) & 63][:coeffs], panel[(right >> 5) & 63][:coeffs]], axis=1)
        made = jnp.dot(operators[left & 31], both, preferred_element_type=jnp.float32)
        return made, left >> 11, right >> 11

    def put(made, left, right):
        total[left, :coeffs] += made[:, :128]
        total[right, :coeffs] += made[:, 128:]

    for size in GROUPS:

        def step(k, carry, first=first, size=size):
            for part in [one(first + k * size + u) for u in range(size)]:
                put(*part)
            return carry

        full = lax.div(last - first, size)
        lax.fori_loop(0, full, step, 0)
        first = first + full * size


def spread_kernel(block, out):
    coeffs = block.shape[0]
    whole = coeffs // 16 * 16
    last = jnp.concatenate([block[whole:], jnp.zeros((out.shape[1] - coeffs, block.shape[1]), block.dtype)], axis=0)
    for t in range(out.shape[0]):
        out[t, :whole] = block[:whole]
        out[t, whole:] = last


def near_kernel(items, ends, operators, own_panel, other_panel, total):
    total[...] = jnp.zeros_like(total)
    add_items(items, 0, ends[0], operators, own_panel, total)
    add_items(items, ends[0], ends[1], operators, other_panel, total)


def far_kernel(items, ends, operators, panel, begun, out, total):
    coeffs = operators.shape[1]
    whole = coeffs // 16 * 16
    total[...] = begun[...]
    add_items(items, ends[1], ends[2], operators, panel, total)

    def code(t):
        values = total[t]
        top = jnp.maximum(jnp.max(jnp.abs(values), axis=0, keepdims=True), 1e-32)
        level = jnp.ceil(jnp.log2(top) * FINE)
        steps = jnp.round(values * jnp.exp2(level * (-1.0 / FINE) + LEVEL_BITS))
        row = lax.broadcasted_iota(jnp.int32, steps[whole:].shape, 0)
        out[t, :whole] = steps[:whole].astype(jnp.int32).astype(jnp.int16)
        out[t, whole:] = jnp.where(row < coeffs - whole, steps[whole:], level).astype(jnp.int32).astype(jnp.int16)

    def some(k, carry):
        for u in range(4):
            code(4 * k + u)
        return carry

    lax.fori_loop(0, out.shape[0] // 4, some, 0)


def sum_kernel(moved, out):
    coeffs = out.shape[0]
    result = jnp.zeros(out.shape, jnp.float32)
    for j in range(moved.shape[0]):
        values = moved[j].astype(jnp.int32).astype(jnp.float32)
        scale = jnp.exp2(values[coeffs : coeffs + 1] * (1.0 / FINE)) * (1.0 / LEVELS)
        result = result + values[:coeffs] * scale
    out[...] = result


def per_device(multipoles, operators, targets, sources, classes, owners):
    own_n = lax.axis_size("own")
    grp_n = lax.axis_size("grp")
    coeffs, width = multipoles.shape
    held = operators.shape[0]
    rows = (coeffs + 16) // 16 * 16
    spread = pl.pallas_call(
        spread_kernel,
        out_shape=jax.ShapeDtypeStruct((own_n, rows, width), multipoles.dtype),
        in_specs=[VMEM],
        out_specs=VMEM,
        compiler_params=pltpu.CompilerParams(vmem_limit_bytes=8 * 2**20),
    )(multipoles)
    own_panel = lax.all_to_all(
        spread, "own", split_axis=0, concat_axis=0, tiled=True
    )
    across = [(i, i + 1) for i in range(1, grp_n - 1, 2)]
    far_panel = lax.ppermute(own_panel, "grp", across + [(j, i) for i, j in across])
    target, sources, classes, owner, unused = lax.optimization_barrier(
        (targets[:, 0], sources, classes, owners[0], own_panel)
    )
    items, ends = plan(target, sources, classes, owner, held)
    other_panel = lax.ppermute(own_panel, "grp", [(i, i ^ 1) for i in range(grp_n)])
    vmem = pltpu.CompilerParams(vmem_limit_bytes=32 * 2**20)
    pair = 2 * coeffs * coeffs * width
    begun = pl.pallas_call(
        near_kernel,
        out_shape=jax.ShapeDtypeStruct((own_n + 1, rows, width), jnp.float32),
        in_specs=[SMEM, SMEM, VMEM, VMEM, VMEM],
        out_specs=VMEM,
        compiler_params=vmem,
        cost_estimate=pl.CostEstimate(flops=pair, bytes_accessed=2**16, transcendentals=0),
    )(items, ends, operators, own_panel, other_panel)
    partial = pl.pallas_call(
        far_kernel,
        out_shape=jax.ShapeDtypeStruct((own_n, rows, width), jnp.int16),
        in_specs=[SMEM, SMEM, VMEM, VMEM, VMEM],
        out_specs=VMEM,
        scratch_shapes=[pltpu.VMEM((own_n + 1, rows, width), jnp.float32)],
        compiler_params=vmem,
        cost_estimate=pl.CostEstimate(flops=3 * 64 * pair, bytes_accessed=2**23, transcendentals=0),
    )(items, ends, operators, far_panel, begun)
    moved = lax.all_to_all(partial, "own", split_axis=0, concat_axis=0, tiled=True)
    return pl.pallas_call(
        sum_kernel,
        out_shape=jax.ShapeDtypeStruct((coeffs, width), jnp.float32),
        in_specs=[VMEM],
        out_specs=VMEM,
        compiler_params=vmem,
    )(moved)


def solution(mesh):
    placed = (
        P(None, ("grp", "own")),
        P("own", None, None),
        P(("grp", "own"), None),
        P(("grp", "own")),
        P(("grp", "own")),
        P("grp", None),
    )
    return jax.shard_map(
        per_device, mesh=mesh, in_specs=placed, out_specs=P(None, ("grp", "own")), check_vma=False
    )
```

```python
import math

import jax
import jax.numpy as jnp
from jax import lax
from jax.experimental import pallas as pl
from jax.experimental.pallas import tpu as pltpu
from jax.sharding import PartitionSpec as P

GROUPS = (16, 4, 1)
SLOTS = 256
LEVELS = 32000.0
LEVEL_BITS = math.log2(LEVELS)
FINE = 64.0
VMEM = pl.BlockSpec(memory_space=pltpu.VMEM)
SMEM = pl.BlockSpec(memory_space=pltpu.SMEM)


def plan(target, sources, classes, owners, held):
    count = target.shape[0]
    own_n = owners.shape[0]
    odd = lax.rem(lax.axis_index("grp"), 2)
    shift = sources % 3
    kind = jnp.where(shift == 1, 0, jnp.where((shift == 0) == (odd == 0), 2, 1))
    local = classes - lax.axis_index("own") * held
    dest = jnp.sum(jnp.where(target[:, None] == jnp.arange(own_n)[None, :], owners[None, :], 0), axis=1)
    packed = local + 32 * (sources // 3) + 2048 * dest
    run = kind * held + local
    pos = jnp.arange(count)
    rank = jnp.sum((run[:, None] == run[None, :]) & (pos[None, :] < pos[:, None]), axis=1, dtype=jnp.int32)
    runs = jnp.arange(3 * held)
    length = jnp.sum(run[:, None] == runs[None, :], axis=0, dtype=jnp.int32)
    length = (length + 1) // 2 * 2
    offset = jnp.sum(jnp.where(runs[None, :] < run[:, None], length[None, :], 0), axis=1)
    slot = offset + rank
    empty = 2048 * own_n
    items = empty + jnp.sum(jnp.where(slot[None, :] == jnp.arange(SLOTS)[:, None], packed[None, :] - empty, 0), axis=1)
    ends = jnp.sum(jnp.where(runs[None, :] < held * jnp.arange(1, 4)[:, None], length[None, :], 0), axis=1) // 2
    return items.astype(jnp.int32), ends.astype(jnp.int32)


def add_items(items, first, last, operators, panel, total, ready=lambda i, seen: seen):
    coeffs = operators.shape[1]

    def one(i):
        left, right = items[2 * i], items[2 * i + 1]
        both = jnp.concatenate([panel[(left >> 5) & 63][:coeffs], panel[(right >> 5) & 63][:coeffs]], axis=1)
        made = jnp.dot(operators[left & 31], both, preferred_element_type=jnp.float32)
        return made, left >> 11, right >> 11

    def put(made, left, right):
        total[left, :coeffs] += made[:, :128]
        total[right, :coeffs] += made[:, 128:]

    seen = jnp.int32(0)
    for size in GROUPS:

        def step(k, seen, first=first, size=size):
            base = first + k * size
            seen = ready(base + size - 1, seen)
            for part in [one(base + u) for u in range(size)]:
                put(*part)
            return seen

        full = lax.div(last - first, size)
        seen = lax.fori_loop(0, full, step, seen)
        first = first + full * size
    return seen


def spread_kernel(block, out):
    coeffs = block.shape[0]
    whole = coeffs // 16 * 16
    last = jnp.concatenate([block[whole:], jnp.zeros((out.shape[1] - coeffs, block.shape[1]), block.dtype)], axis=0)
    for t in range(out.shape[0]):
        out[t, :whole] = block[:whole]
        out[t, whole:] = last


def near_kernel(items, ends, held, own_panel, other_panel, total, operators, arrived):
    def copy(c):
        return pltpu.make_async_copy(held.at[c], operators.at[c], arrived.at[c])

    def wait(c, carry):
        copy(c).wait()
        return carry

    def ready(i, seen):
        need = (items[2 * i] & 31) + 1
        lax.fori_loop(seen, need, wait, 0)
        return jnp.maximum(seen, need)

    for c in range(held.shape[0]):
        copy(c).start()
    total[...] = jnp.zeros_like(total)
    seen = add_items(items, 0, ends[0], operators, own_panel, total, ready)
    lax.fori_loop(seen, held.shape[0], wait, 0)
    add_items(items, ends[0], ends[1], operators, other_panel, total)


def far_kernel(items, ends, operators, panel, begun, out, total):
    coeffs = operators.shape[1]
    whole = coeffs // 16 * 16
    total[...] = begun[...]
    add_items(items, ends[1], ends[2], operators, panel, total)

    def code(t):
        values = total[t]
        top = jnp.maximum(jnp.max(jnp.abs(values), axis=0, keepdims=True), 1e-32)
        level = jnp.ceil(jnp.log2(top) * FINE)
        steps = jnp.round(values * jnp.exp2(level * (-1.0 / FINE) + LEVEL_BITS))
        row = lax.broadcasted_iota(jnp.int32, steps[whole:].shape, 0)
        out[t, :whole] = steps[:whole].astype(jnp.int32).astype(jnp.int16)
        out[t, whole:] = jnp.where(row < coeffs - whole, steps[whole:], level).astype(jnp.int32).astype(jnp.int16)

    def some(k, carry):
        for u in range(4):
            code(4 * k + u)
        return carry

    lax.fori_loop(0, out.shape[0] // 4, some, 0)


def sum_kernel(moved, out):
    coeffs = out.shape[0]
    result = jnp.zeros(out.shape, jnp.float32)
    for j in range(moved.shape[0]):
        values = moved[j].astype(jnp.int32).astype(jnp.float32)
        scale = jnp.exp2(values[coeffs : coeffs + 1] * (1.0 / FINE)) * (1.0 / LEVELS)
        result = result + values[:coeffs] * scale
    out[...] = result


def per_device(multipoles, operators, targets, sources, classes, owners):
    own_n = lax.axis_size("own")
    grp_n = lax.axis_size("grp")
    coeffs, width = multipoles.shape
    held = operators.shape[0]
    rows = (coeffs + 8) // 8 * 8
    spread = pl.pallas_call(
        spread_kernel,
        out_shape=jax.ShapeDtypeStruct((own_n, rows, width), multipoles.dtype),
        in_specs=[VMEM],
        out_specs=VMEM,
        compiler_params=pltpu.CompilerParams(vmem_limit_bytes=8 * 2**20),
    )(pltpu.with_memory_space_constraint(multipoles, pltpu.HBM))
    own_panel = lax.all_to_all(
        spread, "own", split_axis=0, concat_axis=0, tiled=True
    )
    across = [(i, i + 1) for i in range(1, grp_n - 1, 2)]
    far_panel = lax.ppermute(own_panel, "grp", across + [(j, i) for i, j in across])
    target, sources, classes, owner, gathered = lax.optimization_barrier(
        (targets[:, 0], sources, classes, owners[0], own_panel)
    )
    items, ends = plan(target, sources, classes, owner, held)
    other_panel = lax.ppermute(gathered, "grp", [(i, i ^ 1) for i in range(grp_n)])
    vmem = pltpu.CompilerParams(vmem_limit_bytes=32 * 2**20)
    pair = 2 * coeffs * coeffs * width
    kept = pltpu.with_memory_space_constraint(operators, pltpu.HBM)
    begun = pl.pallas_call(
        near_kernel,
        out_shape=jax.ShapeDtypeStruct((own_n + 1, rows, width), jnp.float32),
        in_specs=[SMEM, SMEM, pl.BlockSpec(memory_space=pltpu.HBM), VMEM, VMEM],
        out_specs=VMEM,
        scratch_shapes=[pltpu.VMEM(operators.shape, operators.dtype), pltpu.SemaphoreType.DMA((held,))],
        compiler_params=vmem,
        cost_estimate=pl.CostEstimate(flops=pair, bytes_accessed=2**16, transcendentals=0),
    )(items, ends, kept, gathered, other_panel)
    partial = pl.pallas_call(
        far_kernel,
        out_shape=jax.ShapeDtypeStruct((own_n, rows, width), jnp.int16),
        in_specs=[SMEM, SMEM, VMEM, VMEM, VMEM],
        out_specs=VMEM,
        scratch_shapes=[pltpu.VMEM((own_n + 1, rows, width), jnp.float32)],
        compiler_params=vmem,
        cost_estimate=pl.CostEstimate(flops=3 * 64 * pair, bytes_accessed=2**23, transcendentals=0),
    )(items, ends, operators, far_panel, begun)
    moved = lax.all_to_all(partial, "own", split_axis=0, concat_axis=0, tiled=True)
    return pl.pallas_call(
        sum_kernel,
        out_shape=jax.ShapeDtypeStruct((coeffs, width), jnp.float32),
        in_specs=[VMEM],
        out_specs=VMEM,
        compiler_params=vmem,
    )(moved)


def solution(mesh):
    placed = (
        P(None, ("grp", "own")),
        P("own", None, None),
        P(("grp", "own"), None),
        P(("grp", "own")),
        P(("grp", "own")),
        P("grp", None),
    )
    return jax.shard_map(
        per_device, mesh=mesh, in_specs=placed, out_specs=P(None, ("grp", "own")), check_vma=False
    )
```

```python
import math

import jax
import jax.numpy as jnp
import numpy as np
from jax import lax
from jax.experimental import pallas as pl
from jax.experimental.pallas import tpu as pltpu
from jax.sharding import PartitionSpec as P

GROUPS = (16, 4, 1)
SLOTS = 256
LEVELS = 32000.0
LEVEL_BITS = math.log2(LEVELS)
FINE = 64.0
VMEM = pl.BlockSpec(memory_space=pltpu.VMEM)
SMEM = pl.BlockSpec(memory_space=pltpu.SMEM)


def plan(target, sources, classes, owners, held):
    count = target.shape[0]
    own_n = owners.shape[0]
    shift = sources % 3
    local = classes % held
    dest = jnp.sum(jnp.where(target[:, None] == jnp.arange(own_n)[None, :], owners[None, :], 0), axis=1)
    packed = local + 32 * (sources // 3) + 2048 * dest
    run = shift * held + local
    pos = jnp.arange(count)
    rank = jnp.sum((run[:, None] == run[None, :]) & (pos[None, :] < pos[:, None]), axis=1, dtype=jnp.int32)
    runs = jnp.arange(3 * held)
    length = jnp.sum(run[:, None] == runs[None, :], axis=0, dtype=jnp.int32)
    length = (length + 1) // 2 * 2
    offset = jnp.sum(jnp.where(runs[None, :] < run[:, None], length[None, :], 0), axis=1)
    slot = offset + rank
    empty = 2048 * own_n
    items = empty + jnp.sum(jnp.where(slot[None, :] == jnp.arange(SLOTS)[:, None], packed[None, :] - empty, 0), axis=1)
    ends = jnp.sum(jnp.where(runs[None, :] < np.array([[held], [2 * held], [3 * held]], np.int32), length[None, :], 0), axis=1) // 2
    return items.astype(jnp.int32), ends.astype(jnp.int32)


def add_items(items, first, last, operators, panel, total):
    coeffs = operators.shape[1]

    def one(i):
        left, right = items[2 * i], items[2 * i + 1]
        both = jnp.concatenate([panel[(left >> 5) & 63][:coeffs], panel[(right >> 5) & 63][:coeffs]], axis=1)
        made = jnp.dot(operators[left & 31], both, preferred_element_type=jnp.float32)
        return made, left >> 11, right >> 11

    def put(made, left, right):
        total[left, :coeffs] += made[:, :128]
        total[right, :coeffs] += made[:, 128:]

    for size in GROUPS:

        def step(k, carry, first=first, size=size):
            for part in [one(first + k * size + u) for u in range(size)]:
                put(*part)
            return carry

        full = lax.div(last - first, size)
        lax.fori_loop(0, full, step, 0)
        first = first + full * size


def spread_kernel(block, out):
    coeffs = block.shape[0]
    whole = coeffs // 16 * 16
    last = jnp.concatenate([block[whole:], jnp.zeros((out.shape[1] - coeffs, block.shape[1]), block.dtype)], axis=0)
    for t in range(out.shape[0]):
        out[t, :whole] = block[:whole]
        out[t, whole:] = last


def ranges(ends):
    odd = lax.rem(lax.axis_index("grp"), 2) == 1
    low, high = (jnp.int32(0), ends[0]), (ends[1], ends[2])
    other = [jnp.where(odd, x, y) for x, y in zip(low, high)]
    far = [jnp.where(odd, y, x) for x, y in zip(low, high)]
    return (ends[0], ends[1]), other, far


def near_kernel(items, ends, operators, own_panel, other_panel, total):
    own, other, far = ranges(ends)
    total[...] = jnp.zeros_like(total)
    add_items(items, *own, operators, own_panel, total)
    add_items(items, *other, operators, other_panel, total)


def far_kernel(items, ends, operators, panel, begun, out, total):
    coeffs = operators.shape[1]
    whole = coeffs // 16 * 16
    total[...] = begun[...]
    own, other, far = ranges(ends)
    add_items(items, *far, operators, panel, total)

    def code(t):
        values = total[t]
        top = jnp.maximum(jnp.max(jnp.abs(values), axis=0, keepdims=True), 1e-32)
        level = jnp.ceil(jnp.log2(top) * FINE)
        steps = jnp.round(values * jnp.exp2(level * (-1.0 / FINE) + LEVEL_BITS))
        row = lax.broadcasted_iota(jnp.int32, steps[whole:].shape, 0)
        out[t, :whole] = steps[:whole].astype(jnp.int32).astype(jnp.int16)
        out[t, whole:] = jnp.where(row < coeffs - whole, steps[whole:], level).astype(jnp.int32).astype(jnp.int16)

    def some(k, carry):
        for u in range(4):
            code(4 * k + u)
        return carry

    lax.fori_loop(0, out.shape[0] // 4, some, 0)


def sum_kernel(moved, out):
    coeffs = out.shape[0]
    result = jnp.zeros(out.shape, jnp.float32)
    for j in range(moved.shape[0]):
        values = moved[j].astype(jnp.int32).astype(jnp.float32)
        scale = jnp.exp2(values[coeffs : coeffs + 1] * (1.0 / FINE)) * (1.0 / LEVELS)
        result = result + values[:coeffs] * scale
    out[...] = result


def per_device(multipoles, operators, targets, sources, classes, owners):
    own_n = lax.axis_size("own")
    grp_n = lax.axis_size("grp")
    coeffs, width = multipoles.shape
    held = operators.shape[0]
    rows = (coeffs + 8) // 8 * 8
    spread = pl.pallas_call(
        spread_kernel,
        out_shape=jax.ShapeDtypeStruct((own_n, rows, width), multipoles.dtype),
        in_specs=[VMEM],
        out_specs=VMEM,
        compiler_params=pltpu.CompilerParams(vmem_limit_bytes=8 * 2**20),
    )(pltpu.with_memory_space_constraint(multipoles, pltpu.HBM))
    own_panel = lax.all_to_all(
        spread, "own", split_axis=0, concat_axis=0, tiled=True
    )
    across = [(i, i + 1) for i in range(1, grp_n - 1, 2)]
    far_panel = lax.ppermute(own_panel, "grp", across + [(j, i) for i, j in across])
    target, sources, classes, owner, gathered = lax.optimization_barrier(
        (targets[:, 0], sources, classes, owners[0], own_panel)
    )
    items, ends = plan(target, sources, classes, owner, held)
    other_panel = lax.ppermute(gathered, "grp", [(i, i ^ 1) for i in range(grp_n)])
    vmem = pltpu.CompilerParams(vmem_limit_bytes=32 * 2**20)
    pair = 2 * coeffs * coeffs * width
    begun = pl.pallas_call(
        near_kernel,
        out_shape=jax.ShapeDtypeStruct((own_n + 1, rows, width), jnp.float32),
        in_specs=[SMEM, SMEM, VMEM, VMEM, VMEM],
        out_specs=VMEM,
        compiler_params=vmem,
        cost_estimate=pl.CostEstimate(flops=pair, bytes_accessed=2**16, transcendentals=0),
    )(items, ends, operators, gathered, other_panel)
    partial = pl.pallas_call(
        far_kernel,
        out_shape=jax.ShapeDtypeStruct((own_n, rows, width), jnp.int16),
        in_specs=[SMEM, SMEM, VMEM, VMEM, VMEM],
        out_specs=VMEM,
        scratch_shapes=[pltpu.VMEM((own_n + 1, rows, width), jnp.float32)],
        compiler_params=vmem,
        cost_estimate=pl.CostEstimate(flops=3 * 64 * pair, bytes_accessed=2**23, transcendentals=0),
    )(items, ends, operators, far_panel, begun)
    moved = lax.all_to_all(partial, "own", split_axis=0, concat_axis=0, tiled=True)
    return pl.pallas_call(
        sum_kernel,
        out_shape=jax.ShapeDtypeStruct((coeffs, width), jnp.float32),
        in_specs=[VMEM],
        out_specs=VMEM,
        compiler_params=vmem,
    )(moved)


def solution(mesh):
    placed = (
        P(None, ("grp", "own")),
        P("own", None, None),
        P(("grp", "own"), None),
        P(("grp", "own")),
        P(("grp", "own")),
        P("grp", None),
    )
    return jax.shard_map(
        per_device, mesh=mesh, in_specs=placed, out_specs=P(None, ("grp", "own")), check_vma=False
    )
```

```python
import math

import jax
import jax.numpy as jnp
import numpy as np
from jax import lax
from jax.experimental import pallas as pl
from jax.experimental.pallas import tpu as pltpu
from jax.sharding import PartitionSpec as P

GROUPS = (16, 8, 4, 2, 1)
SLOTS = 256
LEVELS = 32000.0
LEVEL_BITS = math.log2(LEVELS)
FINE = 64.0
VMEM = pl.BlockSpec(memory_space=pltpu.VMEM)
SMEM = pl.BlockSpec(memory_space=pltpu.SMEM)


def plan(target, sources, classes, owners, held):
    count = target.shape[0]
    own_n = owners.shape[0]
    shift = sources % 3
    local = classes % held
    dest = jnp.sum(jnp.where(target[:, None] == jnp.arange(own_n)[None, :], owners[None, :], 0), axis=1)
    packed = local + 32 * (sources // 3) + 2048 * dest
    run = shift * held + local
    pos = jnp.arange(count)
    rank = jnp.sum((run[:, None] == run[None, :]) & (pos[None, :] < pos[:, None]), axis=1, dtype=jnp.int32)
    runs = jnp.arange(3 * held)
    length = jnp.sum(run[:, None] == runs[None, :], axis=0, dtype=jnp.int32)
    length = (length + 1) // 2 * 2
    offset = jnp.sum(jnp.where(runs[None, :] < run[:, None], length[None, :], 0), axis=1)
    slot = offset + rank
    empty = 2048 * own_n
    items = empty + jnp.sum(jnp.where(slot[None, :] == jnp.arange(SLOTS)[:, None], packed[None, :] - empty, 0), axis=1)
    ends = jnp.sum(jnp.where(runs[None, :] < np.array([[held], [2 * held], [3 * held]], np.int32), length[None, :], 0), axis=1) // 2
    return items.astype(jnp.int32), ends.astype(jnp.int32)


def add_items(items, first, last, operators, panel, total):
    coeffs = operators.shape[1]

    def one(i):
        left, right = items[2 * i], items[2 * i + 1]
        both = jnp.concatenate([panel[(left >> 5) & 63][:coeffs], panel[(right >> 5) & 63][:coeffs]], axis=1)
        made = jnp.dot(operators[left & 31], both, preferred_element_type=jnp.float32)
        return made, left >> 11, right >> 11

    def put(made, left, right):
        total[left, :coeffs] += made[:, :128]
        total[right, :coeffs] += made[:, 128:]

    for size in GROUPS:

        def step(k, carry, first=first, size=size):
            for part in [one(first + k * size + u) for u in range(size)]:
                put(*part)
            return carry

        full = lax.div(last - first, size)
        lax.fori_loop(0, full, step, 0)
        first = first + full * size


def spread_kernel(block, out):
    coeffs = block.shape[0]
    whole = coeffs // 16 * 16
    last = jnp.concatenate([block[whole:], jnp.zeros((out.shape[1] - coeffs, block.shape[1]), block.dtype)], axis=0)
    for t in range(out.shape[0]):
        out[t, :whole] = block[:whole]
        out[t, whole:] = last


def ranges(ends):
    odd = lax.rem(lax.axis_index("grp"), 2) == 1
    low, high = (jnp.int32(0), ends[0]), (ends[1], ends[2])
    other = [jnp.where(odd, x, y) for x, y in zip(low, high)]
    far = [jnp.where(odd, y, x) for x, y in zip(low, high)]
    return (ends[0], ends[1]), other, far


def copy_kernel(panel, out):
    for t in range(out.shape[0]):
        out[t] = panel[t]


def near_kernel(items, ends, operators, own_panel, other_panel, total):
    own, other, far = ranges(ends)
    total[...] = jnp.zeros_like(total)
    add_items(items, *own, operators, own_panel, total)
    add_items(items, *other, operators, other_panel, total)


def far_kernel(items, ends, operators, panel, begun, out, total):
    coeffs = operators.shape[1]
    whole = coeffs // 16 * 16
    total[...] = begun[...]
    own, other, far = ranges(ends)
    add_items(items, *far, operators, panel, total)

    def code(t):
        values = total[t]
        top = jnp.maximum(jnp.max(jnp.abs(values), axis=0, keepdims=True), 1e-32)
        level = jnp.ceil(jnp.log2(top) * FINE)
        steps = jnp.round(values * jnp.exp2(level * (-1.0 / FINE) + LEVEL_BITS))
        row = lax.broadcasted_iota(jnp.int32, steps[whole:].shape, 0)
        out[t, :whole] = steps[:whole].astype(jnp.int32).astype(jnp.int16)
        out[t, whole:] = jnp.where(row < coeffs - whole, steps[whole:], level).astype(jnp.int32).astype(jnp.int16)

    def some(k, carry):
        for u in range(4):
            code(4 * k + u)
        return carry

    lax.fori_loop(0, out.shape[0] // 4, some, 0)


def sum_kernel(moved, out):
    coeffs = out.shape[0]
    result = jnp.zeros(out.shape, jnp.float32)
    for j in range(moved.shape[0]):
        values = moved[j].astype(jnp.int32).astype(jnp.float32)
        scale = jnp.exp2(values[coeffs : coeffs + 1] * (1.0 / FINE)) * (1.0 / LEVELS)
        result = result + values[:coeffs] * scale
    out[...] = result


def per_device(multipoles, operators, targets, sources, classes, owners):
    own_n = lax.axis_size("own")
    grp_n = lax.axis_size("grp")
    coeffs, width = multipoles.shape
    held = operators.shape[0]
    rows = (coeffs + 8) // 8 * 8
    spread = pl.pallas_call(
        spread_kernel,
        out_shape=jax.ShapeDtypeStruct((own_n, rows, width), multipoles.dtype),
        in_specs=[VMEM],
        out_specs=VMEM,
        compiler_params=pltpu.CompilerParams(vmem_limit_bytes=8 * 2**20),
    )(pltpu.with_memory_space_constraint(multipoles, pltpu.HBM))
    own_panel = lax.all_to_all(
        spread, "own", split_axis=0, concat_axis=0, tiled=True
    )
    across = [(i, i + 1) for i in range(1, grp_n - 1, 2)]
    other_panel = lax.ppermute(own_panel, "grp", [(i, i ^ 1) for i in range(grp_n)])
    target, sources, classes, owner, gathered = lax.optimization_barrier(
        (targets[:, 0], sources, classes, owners[0], own_panel)
    )
    items, ends = plan(target, sources, classes, owner, held)
    leaving = pl.pallas_call(
        copy_kernel,
        out_shape=jax.ShapeDtypeStruct(own_panel.shape, own_panel.dtype),
        in_specs=[VMEM],
        out_specs=VMEM,
        compiler_params=pltpu.CompilerParams(vmem_limit_bytes=8 * 2**20),
    )(gathered)
    far_panel = lax.ppermute(leaving, "grp", across + [(j, i) for i, j in across])
    vmem = pltpu.CompilerParams(vmem_limit_bytes=32 * 2**20)
    pair = 2 * coeffs * coeffs * width
    begun = pl.pallas_call(
        near_kernel,
        out_shape=jax.ShapeDtypeStruct((own_n + 1, rows, width), jnp.float32),
        in_specs=[SMEM, SMEM, VMEM, VMEM, VMEM],
        out_specs=VMEM,
        compiler_params=vmem,
        cost_estimate=pl.CostEstimate(flops=pair, bytes_accessed=2**16, transcendentals=0),
    )(items, ends, operators, gathered, other_panel)
    partial = pl.pallas_call(
        far_kernel,
        out_shape=jax.ShapeDtypeStruct((own_n, rows, width), jnp.int16),
        in_specs=[SMEM, SMEM, VMEM, VMEM, VMEM],
        out_specs=VMEM,
        scratch_shapes=[pltpu.VMEM((own_n + 1, rows, width), jnp.float32)],
        compiler_params=vmem,
        cost_estimate=pl.CostEstimate(flops=3 * 64 * pair, bytes_accessed=2**23, transcendentals=0),
    )(items, ends, operators, far_panel, begun)
    moved = lax.all_to_all(partial, "own", split_axis=0, concat_axis=0, tiled=True)
    return pl.pallas_call(
        sum_kernel,
        out_shape=jax.ShapeDtypeStruct((coeffs, width), jnp.float32),
        in_specs=[VMEM],
        out_specs=VMEM,
        compiler_params=vmem,
    )(moved)


def solution(mesh):
    placed = (
        P(None, ("grp", "own")),
        P("own", None, None),
        P(("grp", "own"), None),
        P(("grp", "own")),
        P(("grp", "own")),
        P("grp", None),
    )
    return jax.shard_map(
        per_device, mesh=mesh, in_specs=placed, out_specs=P(None, ("grp", "own")), check_vma=False
    )
```

```python
import math

import jax
import jax.numpy as jnp
import numpy as np
from jax import lax
from jax.experimental import pallas as pl
from jax.experimental.pallas import tpu as pltpu
from jax.sharding import PartitionSpec as P

GROUPS = (16, 8, 4, 2, 1)
SLOTS = 256
CHUNK = 96
LEVELS = 32000.0
LEVEL_BITS = math.log2(LEVELS)
FINE = 64.0
VMEM = pl.BlockSpec(memory_space=pltpu.VMEM)
SMEM = pl.BlockSpec(memory_space=pltpu.SMEM)


def plan(target, sources, classes, owners, held):
    count = target.shape[0]
    own_n = owners.shape[0]
    shift = sources % 3
    local = classes % held
    dest = jnp.sum(jnp.where(target[:, None] == jnp.arange(own_n)[None, :], owners[None, :], 0), axis=1)
    packed = local + 32 * (sources // 3) + 2048 * dest
    run = shift * held + local
    pos = jnp.arange(count)
    rank = jnp.sum((run[:, None] == run[None, :]) & (pos[None, :] < pos[:, None]), axis=1, dtype=jnp.int32)
    runs = jnp.arange(3 * held)
    length = jnp.sum(run[:, None] == runs[None, :], axis=0, dtype=jnp.int32)
    length = (length + 1) // 2 * 2
    offset = jnp.sum(jnp.where(runs[None, :] < run[:, None], length[None, :], 0), axis=1)
    slot = offset + rank
    empty = 2048 * own_n
    items = empty + jnp.sum(jnp.where(slot[None, :] == jnp.arange(SLOTS)[:, None], packed[None, :] - empty, 0), axis=1)
    ends = jnp.sum(jnp.where(runs[None, :] < np.array([[held], [2 * held], [3 * held]], np.int32), length[None, :], 0), axis=1) // 2
    return items.astype(jnp.int32), ends.astype(jnp.int32)


def add_items(items, first, last, operators, panel, total):
    coeffs = operators.shape[1]

    def one(i):
        left, right = items[2 * i], items[2 * i + 1]
        both = jnp.concatenate([panel[(left >> 5) & 63][:coeffs], panel[(right >> 5) & 63][:coeffs]], axis=1)
        made = jnp.dot(operators[left & 31], both, preferred_element_type=jnp.float32)
        return made, left >> 11, right >> 11

    def put(made, left, right):
        total[left, :coeffs] += made[:, :128]
        total[right, :coeffs] += made[:, 128:]

    for size in GROUPS:

        def step(k, carry, first=first, size=size):
            for part in [one(first + k * size + u) for u in range(size)]:
                put(*part)
            return carry

        full = lax.div(last - first, size)
        lax.fori_loop(0, full, step, 0)
        first = first + full * size


def spread_kernel(block, out):
    coeffs = block.shape[0]
    whole = coeffs // 16 * 16
    last = jnp.concatenate([block[whole:], jnp.zeros((out.shape[1] - coeffs, block.shape[1]), block.dtype)], axis=0)
    for t in range(out.shape[0]):
        out[t, :whole] = block[:whole]
        out[t, whole:] = last


def ranges(ends):
    odd = lax.rem(lax.axis_index("grp"), 2) == 1
    low, high = (jnp.int32(0), ends[0]), (ends[1], ends[2])
    other = [jnp.where(odd, x, y) for x, y in zip(low, high)]
    far = [jnp.where(odd, y, x) for x, y in zip(low, high)]
    return (ends[0], ends[1]), other, far


def copy_kernel(panel, out):
    for t in range(out.shape[0]):
        out[t] = panel[t]


def near_kernel(items, ends, operators, own_panel, other_panel, total):
    own, other, far = ranges(ends)
    total[...] = jnp.zeros_like(total)
    add_items(items, *own, operators, own_panel, total)
    add_items(items, *other, operators, other_panel, total)


def far_kernel(items, ends, operators, panel, begun, out, total):
    coeffs = operators.shape[1]
    whole = coeffs // 16 * 16
    total[...] = begun[...]
    own, other, far = ranges(ends)
    add_items(items, *far, operators, panel, total)

    def code(t):
        top = jnp.full((1, out.shape[2]), 1e-32, jnp.float32)
        for low in range(0, whole, CHUNK):
            top = jnp.maximum(top, jnp.max(jnp.abs(total[t, low : low + CHUNK]), axis=0, keepdims=True))
        last = total[t, whole:]
        top = jnp.maximum(top, jnp.max(jnp.abs(last), axis=0, keepdims=True))
        level = jnp.ceil(jnp.log2(top) * FINE)
        scale = jnp.exp2(level * (-1.0 / FINE) + LEVEL_BITS)
        for low in range(0, whole, CHUNK):
            steps = jnp.round(total[t, low : low + CHUNK] * scale)
            out[t, low : low + CHUNK] = steps.astype(jnp.int32).astype(jnp.int16)
        row = lax.broadcasted_iota(jnp.int32, last.shape, 0)
        out[t, whole:] = jnp.where(row < coeffs - whole, jnp.round(last * scale), level).astype(jnp.int32).astype(jnp.int16)

    def some(k, carry):
        for u in range(4):
            code(4 * k + u)
        return carry

    lax.fori_loop(0, out.shape[0] // 4, some, 0)


def sum_kernel(moved, out):
    coeffs = out.shape[0]
    whole = coeffs // 16 * 16
    many = range(moved.shape[0])

    def values(j, low, high):
        return moved[j, low:high].astype(jnp.int32).astype(jnp.float32)

    lasts = [values(j, whole, moved.shape[1]) for j in many]
    scales = [
        jnp.exp2(last[coeffs - whole : coeffs - whole + 1] * (1.0 / FINE)) * (1.0 / LEVELS) for last in lasts
    ]
    for low in range(0, whole, CHUNK):
        result = values(0, low, low + CHUNK) * scales[0]
        for j in many[1:]:
            result = result + values(j, low, low + CHUNK) * scales[j]
        out[low : low + CHUNK] = result
    result = lasts[0][: coeffs - whole] * scales[0]
    for j in many[1:]:
        result = result + lasts[j][: coeffs - whole] * scales[j]
    out[whole:] = result


def per_device(multipoles, operators, targets, sources, classes, owners):
    own_n = lax.axis_size("own")
    grp_n = lax.axis_size("grp")
    coeffs, width = multipoles.shape
    held = operators.shape[0]
    rows = (coeffs + 8) // 8 * 8
    spread = pl.pallas_call(
        spread_kernel,
        out_shape=jax.ShapeDtypeStruct((own_n, rows, width), multipoles.dtype),
        in_specs=[VMEM],
        out_specs=VMEM,
        compiler_params=pltpu.CompilerParams(vmem_limit_bytes=8 * 2**20),
    )(pltpu.with_memory_space_constraint(multipoles, pltpu.HBM))
    own_panel = lax.all_to_all(
        spread, "own", split_axis=0, concat_axis=0, tiled=True
    )
    across = [(i, i + 1) for i in range(1, grp_n - 1, 2)]
    other_panel = lax.ppermute(own_panel, "grp", [(i, i ^ 1) for i in range(grp_n)])
    target, sources, classes, owner, gathered = lax.optimization_barrier(
        (targets[:, 0], sources, classes, owners[0], own_panel)
    )
    items, ends = plan(target, sources, classes, owner, held)
    leaving = pl.pallas_call(
        copy_kernel,
        out_shape=jax.ShapeDtypeStruct(own_panel.shape, own_panel.dtype),
        in_specs=[VMEM],
        out_specs=VMEM,
        compiler_params=pltpu.CompilerParams(vmem_limit_bytes=8 * 2**20),
    )(gathered)
    far_panel = lax.ppermute(leaving, "grp", across + [(j, i) for i, j in across])
    vmem = pltpu.CompilerParams(vmem_limit_bytes=32 * 2**20)
    pair = 2 * coeffs * coeffs * width
    begun = pl.pallas_call(
        near_kernel,
        out_shape=jax.ShapeDtypeStruct((own_n + 1, rows, width), jnp.float32),
        in_specs=[SMEM, SMEM, VMEM, VMEM, VMEM],
        out_specs=VMEM,
        compiler_params=vmem,
        cost_estimate=pl.CostEstimate(flops=pair, bytes_accessed=2**16, transcendentals=0),
    )(items, ends, operators, gathered, other_panel)
    partial = pl.pallas_call(
        far_kernel,
        out_shape=jax.ShapeDtypeStruct((own_n, rows, width), jnp.int16),
        in_specs=[SMEM, SMEM, VMEM, VMEM, VMEM],
        out_specs=VMEM,
        scratch_shapes=[pltpu.VMEM((own_n + 1, rows, width), jnp.float32)],
        compiler_params=vmem,
        cost_estimate=pl.CostEstimate(flops=3 * 64 * pair, bytes_accessed=2**23, transcendentals=0),
    )(items, ends, operators, far_panel, begun)
    moved = lax.all_to_all(partial, "own", split_axis=0, concat_axis=0, tiled=True)
    return pl.pallas_call(
        sum_kernel,
        out_shape=jax.ShapeDtypeStruct((coeffs, width), jnp.float32),
        in_specs=[VMEM],
        out_specs=VMEM,
        compiler_params=vmem,
    )(moved)


def solution(mesh):
    placed = (
        P(None, ("grp", "own")),
        P("own", None, None),
        P(("grp", "own"), None),
        P(("grp", "own")),
        P(("grp", "own")),
        P("grp", None),
    )
    return jax.shard_map(
        per_device, mesh=mesh, in_specs=placed, out_specs=P(None, ("grp", "own")), check_vma=False
    )
```

```python
import math

import jax
import jax.numpy as jnp
import numpy as np
from jax import lax
from jax.experimental import pallas as pl
from jax.experimental.pallas import tpu as pltpu
from jax.sharding import PartitionSpec as P

GROUPS = (16, 8, 4, 2, 1)
SLOTS = 256
CHUNK = 96
LEVELS = 32000.0
LEVEL_BITS = math.log2(LEVELS)
FINE = 64.0
VMEM = pl.BlockSpec(memory_space=pltpu.VMEM)
SMEM = pl.BlockSpec(memory_space=pltpu.SMEM)


def plan(target, sources, classes, owners, held):
    count = target.shape[0]
    own_n = owners.shape[0]
    shift = sources % 3
    local = classes % held
    dest = jnp.sum(jnp.where(target[:, None] == jnp.arange(own_n)[None, :], owners[None, :], 0), axis=1)
    packed = local + 32 * (sources // 3) + 2048 * dest
    run = shift * held + local
    pos = jnp.arange(count)
    rank = jnp.sum((run[:, None] == run[None, :]) & (pos[None, :] < pos[:, None]), axis=1, dtype=jnp.int32)
    runs = jnp.arange(3 * held)
    length = jnp.sum(run[:, None] == runs[None, :], axis=0, dtype=jnp.int32)
    length = (length + 1) // 2 * 2
    offset = jnp.sum(jnp.where(runs[None, :] < run[:, None], length[None, :], 0), axis=1)
    slot = offset + rank
    empty = 2048 * own_n
    items = empty + jnp.sum(jnp.where(slot[None, :] == jnp.arange(SLOTS)[:, None], packed[None, :] - empty, 0), axis=1)
    ends = jnp.sum(jnp.where(runs[None, :] < np.array([[held], [2 * held], [3 * held]], np.int32), length[None, :], 0), axis=1) // 2
    return items.astype(jnp.int32), ends.astype(jnp.int32)


def add_items(items, first, last, operators, panel, total):
    coeffs = operators.shape[1]

    def one(i):
        left, right = items[2 * i], items[2 * i + 1]
        both = jnp.concatenate([panel[(left >> 5) & 63][:coeffs], panel[(right >> 5) & 63][:coeffs]], axis=1)
        made = jnp.dot(operators[left & 31], both, preferred_element_type=jnp.float32)
        return made, left >> 11, right >> 11

    def put(made, left, right):
        total[left, :coeffs] += made[:, :128]
        total[right, :coeffs] += made[:, 128:]

    for size in GROUPS:

        def step(k, carry, first=first, size=size):
            for part in [one(first + k * size + u) for u in range(size)]:
                put(*part)
            return carry

        full = lax.div(last - first, size)
        lax.fori_loop(0, full, step, 0)
        first = first + full * size


def spread_kernel(block, out):
    coeffs = block.shape[0]
    whole = coeffs // 16 * 16
    last = jnp.concatenate([block[whole:], jnp.zeros((out.shape[1] - coeffs, block.shape[1]), block.dtype)], axis=0)
    for t in range(out.shape[0]):
        out[t, :whole] = block[:whole]
        out[t, whole:] = last


def ranges(ends):
    odd = lax.rem(lax.axis_index("grp"), 2) == 1
    low, high = (jnp.int32(0), ends[0]), (ends[1], ends[2])
    other = [jnp.where(odd, x, y) for x, y in zip(low, high)]
    far = [jnp.where(odd, y, x) for x, y in zip(low, high)]
    return (ends[0], ends[1]), other, far


def copy_kernel(panel, out):
    for t in range(out.shape[0]):
        out[t] = panel[t]


def near_kernel(items, ends, operators, own_panel, other_panel, total):
    own, other, far = ranges(ends)
    total[...] = jnp.zeros_like(total)
    add_items(items, *own, operators, own_panel, total)
    add_items(items, *other, operators, other_panel, total)


def far_kernel(items, ends, operators, panel, begun, out, total):
    coeffs = operators.shape[1]
    whole = coeffs // 16 * 16
    total[...] = begun[...]
    own, other, far = ranges(ends)
    add_items(items, *far, operators, panel, total)

    def code(t):
        top = jnp.full((1, out.shape[2]), 1e-32, jnp.float32)
        for low in range(0, whole, CHUNK):
            top = jnp.maximum(top, jnp.max(jnp.abs(total[t, low : low + CHUNK]), axis=0, keepdims=True))
        last = total[t, whole:]
        top = jnp.maximum(top, jnp.max(jnp.abs(last), axis=0, keepdims=True))
        level = jnp.ceil(jnp.log2(top) * FINE)
        scale = jnp.exp2(level * (-1.0 / FINE) + LEVEL_BITS)
        for low in range(0, whole, CHUNK):
            steps = jnp.round(total[t, low : low + CHUNK] * scale)
            out[t, low : low + CHUNK] = steps.astype(jnp.int32).astype(jnp.int16)
        row = lax.broadcasted_iota(jnp.int32, last.shape, 0)
        out[t, whole:] = jnp.where(row < coeffs - whole, jnp.round(last * scale), level).astype(jnp.int32).astype(jnp.int16)

    for t in range(out.shape[0]):
        code(t)


def sum_kernel(moved, out):
    coeffs = out.shape[0]
    whole = coeffs // 16 * 16
    many = range(moved.shape[0])

    def values(j, low, high):
        return moved[j, low:high].astype(jnp.int32).astype(jnp.float32)

    lasts = [values(j, whole, moved.shape[1]) for j in many]
    scales = [
        jnp.exp2(last[coeffs - whole : coeffs - whole + 1] * (1.0 / FINE)) * (1.0 / LEVELS) for last in lasts
    ]
    for low in range(0, whole, CHUNK):
        result = values(0, low, low + CHUNK) * scales[0]
        for j in many[1:]:
            result = result + values(j, low, low + CHUNK) * scales[j]
        out[low : low + CHUNK] = result
    result = lasts[0][: coeffs - whole] * scales[0]
    for j in many[1:]:
        result = result + lasts[j][: coeffs - whole] * scales[j]
    out[whole:] = result


def per_device(multipoles, operators, targets, sources, classes, owners):
    own_n = lax.axis_size("own")
    grp_n = lax.axis_size("grp")
    coeffs, width = multipoles.shape
    held = operators.shape[0]
    rows = (coeffs + 8) // 8 * 8
    spread = pl.pallas_call(
        spread_kernel,
        out_shape=jax.ShapeDtypeStruct((own_n, rows, width), multipoles.dtype),
        in_specs=[VMEM],
        out_specs=VMEM,
        compiler_params=pltpu.CompilerParams(vmem_limit_bytes=8 * 2**20),
    )(pltpu.with_memory_space_constraint(multipoles, pltpu.HBM))
    own_panel = lax.all_to_all(
        spread, "own", split_axis=0, concat_axis=0, tiled=True
    )
    across = [(i, i + 1) for i in range(1, grp_n - 1, 2)]
    other_panel = lax.ppermute(own_panel, "grp", [(i, i ^ 1) for i in range(grp_n)])
    target, sources, classes, owner, gathered = lax.optimization_barrier(
        (targets[:, 0], sources, classes, owners[0], own_panel)
    )
    items, ends = plan(target, sources, classes, owner, held)
    leaving = pl.pallas_call(
        copy_kernel,
        out_shape=jax.ShapeDtypeStruct(own_panel.shape, own_panel.dtype),
        in_specs=[VMEM],
        out_specs=VMEM,
        compiler_params=pltpu.CompilerParams(vmem_limit_bytes=8 * 2**20),
    )(gathered)
    far_panel = lax.ppermute(leaving, "grp", across + [(j, i) for i, j in across])
    vmem = pltpu.CompilerParams(vmem_limit_bytes=32 * 2**20)
    pair = 2 * coeffs * coeffs * width
    begun = pl.pallas_call(
        near_kernel,
        out_shape=jax.ShapeDtypeStruct((own_n + 1, rows, width), jnp.float32),
        in_specs=[SMEM, SMEM, VMEM, VMEM, VMEM],
        out_specs=VMEM,
        compiler_params=vmem,
        cost_estimate=pl.CostEstimate(flops=pair, bytes_accessed=2**16, transcendentals=0),
    )(items, ends, operators, gathered, other_panel)
    partial = pl.pallas_call(
        far_kernel,
        out_shape=jax.ShapeDtypeStruct((own_n, rows, width), jnp.int16),
        in_specs=[SMEM, SMEM, VMEM, VMEM, VMEM],
        out_specs=VMEM,
        scratch_shapes=[pltpu.VMEM((own_n + 1, rows, width), jnp.float32)],
        compiler_params=vmem,
        cost_estimate=pl.CostEstimate(flops=3 * 64 * pair, bytes_accessed=2**23, transcendentals=0),
    )(items, ends, operators, far_panel, begun)
    moved = lax.all_to_all(partial, "own", split_axis=0, concat_axis=0, tiled=True)
    return pl.pallas_call(
        sum_kernel,
        out_shape=jax.ShapeDtypeStruct((coeffs, width), jnp.float32),
        in_specs=[VMEM],
        out_specs=VMEM,
        compiler_params=vmem,
    )(moved)


def solution(mesh):
    placed = (
        P(None, ("grp", "own")),
        P("own", None, None),
        P(("grp", "own"), None),
        P(("grp", "own")),
        P(("grp", "own")),
        P("grp", None),
    )
    return jax.shard_map(
        per_device, mesh=mesh, in_specs=placed, out_specs=P(None, ("grp", "own")), check_vma=False
    )
```
